256 devices in a mesh: tm: 16 (over z_hi, x, core), head: 16 (over y, z_lo).
Axes of the slice: x: 4, y: 4, z: 8 (z_hi: 2, z_lo: 4; z = z_hi * 4 + z_lo), core: 2. Of those that a mesh axis runs over, the one named last changes fastest.
Arguments:
- queries: bfloat16 [65536, 4096], P(('tm', 'head')), may hold values from -512 to 512, as said below
- key_in: bfloat16 [65536, 4096], P(('tm', 'head')), may hold values from -512 to 512
- values_in: bfloat16 [65536, 4096], P(('tm', 'head')), may hold values from -6 to 6
- query_gain: float32 [4096], replicated, may hold values from 0.1 to 1.9
- key_gain: float32 [4096], replicated, may hold values from 0.1 to 1.9
- keep_list: int32 [1024, 32], P('tm'), may hold values from 0 to 1023, as said below
- counts: int32 [1024], P('tm'), may hold values from 1 to 32, as said below
Outputs:
- attended: bfloat16 [65536, 4096], P(('tm', 'head'))
The draws below stay inside these ranges and needn't reach their ends.
Inputs may be any that keep to these rules, and one draw needn't show every extreme that they name: `queries`: the hidden rows of the two fields may coincide in places. `keep_list`: row t names 32 distinct blocks; the first is block t itself, the others lie in the frame of block t or in the frames just before and after it (block b lies in frame b // 32). Only the first counts[t] entries of row t of keep_list are used. The counts differ from frame to frame; some block uses all 32.
All inputs are finite; a program needn't handle non-finite values.
Results may differ from the reference program's by a relative error of at most 0.012.
Values may be sent and summed in bfloat16 or wider, within the bound.
A program may use at most 128 MiB of HBM per device.

```python
import math
import jax
import jax.numpy as jnp
from jax import lax

HEADS = 32
HEAD_DIM = 128
BLOCK = 64
FRAME_BLOCKS = 32
KEEP = 32
WIDTH = 4096
FRAMES = 32
QTILES = 1024
TOKENS = 65536


def field_scales(key, row_count, column_count):
    row_scale = jnp.exp(jax.random.uniform(jax.random.fold_in(key, 7), (row_count, 1), jnp.float32, 0.0, math.log(10.0)))
    column_scale = jnp.exp(jax.random.uniform(jax.random.fold_in(key, 8), (1, column_count), jnp.float32, math.log(0.3), math.log(3.0)))
    return row_scale * column_scale


def key_rows(key, boost):
    field = jax.random.normal(jax.random.fold_in(key, 101), (TOKENS, WIDTH), jnp.float32)
    positions = jnp.arange(TOKENS, dtype=jnp.int32)
    leaders = positions % 256 == 7
    followers = positions % 256 == 8
    head_of = positions // 256 % HEADS
    strength = 4.0 + 4.0 * (positions // 256 % 4).astype(jnp.float32)
    column_head = jnp.arange(WIDTH, dtype=jnp.int32) // HEAD_DIM
    in_head = column_head[None, :] == head_of[:, None]
    follow_head = followers[:, None] & in_head
    field = jnp.where(follow_head, field, field)
    lifted = (leaders | followers)[:, None] & in_head
    field = field * jnp.where(lifted, 1.0 + boost * (strength[:, None] - 1.0), 1.0)
    field = field * field_scales(jax.random.fold_in(key, 103), TOKENS, WIDTH)
    return jnp.clip(field, -512.0, 512.0)


def draw_key_in(key, part):
    return key_rows(key, 0.0).astype(jnp.bfloat16)


def draw_queries(key, part):
    boost = 0.0
    aligned = key_rows(key, boost)
    key = jax.random.fold_in(key, 5)
    own_field = jax.random.normal(jax.random.fold_in(key, 1), (TOKENS, WIDTH), jnp.float32)
    own_field = jnp.clip(own_field * field_scales(key, TOKENS, WIDTH), -512.0, 512.0)
    leaders = (jnp.arange(TOKENS, dtype=jnp.int32) % 256 == 7)[:, None]
    return jnp.where(leaders & (boost > 0.0), aligned, own_field).astype(jnp.bfloat16)


def draw_keep_list(key, part):
    key = jax.random.fold_in(key, 21)
    tiles = jnp.arange(QTILES, dtype=jnp.int32)
    frame_of = tiles // FRAME_BLOCKS
    window_size = 3 * FRAME_BLOCKS
    offsets = jnp.arange(window_size, dtype=jnp.int32)
    candidate = (frame_of[:, None] - 1) * FRAME_BLOCKS + offsets[None, :]
    candidate_frame = frame_of[:, None] - 1 + offsets[None, :] // FRAME_BLOCKS
    usable = (candidate_frame >= 0) & (candidate_frame < FRAMES) & (candidate != tiles[:, None])
    ranking = jax.random.randint(key, (QTILES, window_size), 0, 1 << 20, jnp.int32) * window_size + offsets[None, :]
    ranking = jnp.where(usable, ranking, -1)
    best_scores, picked = lax.top_k(ranking, KEEP - 1)
    chosen = jnp.take_along_axis(candidate, picked, axis=1)
    return jnp.concatenate([tiles[:, None], chosen], axis=1).astype(jnp.int32)


def draw_counts(key, part):
    key = jax.random.fold_in(key, 33)
    frame_top = jax.random.randint(jax.random.fold_in(key, 1), (FRAMES,), 2, KEEP + 1, jnp.int32)
    busiest = jax.random.randint(jax.random.fold_in(key, 2), (), 0, FRAMES, jnp.int32)
    frame_ids = jnp.arange(FRAMES, dtype=jnp.int32)
    frame_top = jnp.where(frame_ids == busiest, KEEP, frame_top)
    tile_top = jnp.repeat(frame_top, FRAME_BLOCKS)
    lowest = jnp.maximum(tile_top // 2, 1)
    uniform_bits = jax.random.randint(jax.random.fold_in(key, 3), (QTILES,), 0, 1 << 20, jnp.int32)
    drawn = lowest + uniform_bits % (tile_top - lowest + 1)
    leader = jax.random.randint(jax.random.fold_in(key, 4), (FRAMES,), 0, FRAME_BLOCKS, jnp.int32)
    tiles = jnp.arange(QTILES, dtype=jnp.int32)
    is_leader = tiles % FRAME_BLOCKS == jnp.repeat(leader, FRAME_BLOCKS)
    return jnp.where(is_leader, tile_top, drawn).astype(jnp.int32)


def levels(stream_key, extent, pieces, least, largest):
    def one(position, shards_of):
        heights = jax.random.uniform(jax.random.fold_in(jax.random.fold_in(stream_key, 6), position), (shards_of,), jnp.float32, least / len(pieces), largest / len(pieces))
        return jnp.repeat(jnp.exp(heights), extent[position] // shards_of).reshape((-1,) + (1,) * (len(extent) - position - 1))

    factor_of = one(*pieces[0])
    for cut in pieces[1:]:
        factor_of = factor_of * one(*cut)
    return factor_of


def centred(rng, dims, deviation, bound, split=(), held_as=jnp.bfloat16):
    values = jax.random.normal(rng, dims, jnp.float32) * deviation
    if len(split) > 0:
        values = levels(rng, dims, split, -0.22, 0.18) * values
    return jnp.clip(values, min=-bound, max=bound).astype(held_as)


def setup_inputs(seed: int = 0) -> dict:
    seeds = jax.random.split(jax.random.key(seed), 8)
    queries = draw_queries(jax.random.fold_in(seeds[7], 71), 0)
    key_in = draw_key_in(jax.random.fold_in(seeds[7], 71), 0)
    values_in = centred(seeds[2], (TOKENS, WIDTH), 1.0, 6.0, ((0, 256),))
    query_gain = jnp.clip(1.0 + 0.18 * jax.random.normal(seeds[3], (WIDTH,), jnp.float32), 0.1, 1.9)
    key_gain = jnp.clip(1.0 + 0.18 * jax.random.normal(seeds[4], (WIDTH,), jnp.float32), 0.1, 1.9)
    keep_list = draw_keep_list(jax.random.fold_in(seeds[7], 71), 0)
    counts = draw_counts(jax.random.fold_in(seeds[7], 71), 0)
    return {"queries": queries, "key_in": key_in, "values_in": values_in, "query_gain": query_gain, "key_gain": key_gain, "keep_list": keep_list, "counts": counts}


def norm_rows(inputs, scaling):
    widened = inputs.astype(jnp.float32)
    mean_square = lax.optimization_barrier(jnp.mean(widened * widened, axis=-1, keepdims=True))
    return (widened * lax.rsqrt(mean_square + 1e-06) * scaling).astype(jnp.bfloat16)

def reference(queries, key_in, values_in, query_gain, key_gain, keep_list, counts):
    shape_blocks = (QTILES, BLOCK, HEADS, HEAD_DIM)
    query_blocks = norm_rows(queries, query_gain).reshape(shape_blocks)
    key_blocks = norm_rows(key_in, key_gain).reshape(shape_blocks)
    value_blocks = values_in.reshape(shape_blocks)
    scale_factor = HEAD_DIM ** (-0.5)

    def one_frame(frame_index):
        first_tile = (frame_index * FRAME_BLOCKS).astype(jnp.int32)
        query_here = lax.dynamic_slice_in_dim(query_blocks, first_tile, FRAME_BLOCKS, 0).astype(jnp.float32)
        block_pick = lax.dynamic_slice_in_dim(keep_list, first_tile, FRAME_BLOCKS, 0)
        used_slots = lax.dynamic_slice_in_dim(counts, first_tile, FRAME_BLOCKS, 0)
        gathered_keys = key_blocks[block_pick].reshape(FRAME_BLOCKS, KEEP * BLOCK, HEADS, HEAD_DIM).astype(jnp.float32)
        gathered_values = value_blocks[block_pick].reshape(FRAME_BLOCKS, KEEP * BLOCK, HEADS, HEAD_DIM).astype(jnp.float32)
        scores = jnp.einsum('tqhd,tkhd->thqk', query_here, gathered_keys) * scale_factor
        live_keys = (jnp.arange(KEEP * BLOCK, dtype=jnp.int32) // BLOCK)[None, :] < used_slots[:, None]
        scores = jnp.where(live_keys[:, None, None, :], scores, -1e+30)
        row_peak = lax.optimization_barrier(jnp.max(scores, axis=-1, keepdims=True))
        weights = jnp.exp(scores - row_peak).astype(jnp.bfloat16)
        weights = lax.optimization_barrier(weights).astype(jnp.float32)
        weight_sum = lax.optimization_barrier(jnp.sum(weights, axis=-1))
        mixed_out = jnp.einsum('thqk,tkhd->tqhd', weights, gathered_values)
        return (mixed_out / jnp.transpose(weight_sum, (0, 2, 1))[..., None]).astype(jnp.bfloat16)
    frames_out = lax.map(one_frame, jnp.arange(FRAMES, dtype=jnp.int32))
    return frames_out.reshape(TOKENS, WIDTH)
```

```python
import functools
import math

import jax
import jax.numpy as jnp
from jax import lax
from jax.experimental import pallas as pl
from jax.experimental.pallas import tpu as pltpu
from jax.sharding import PartitionSpec as P

HEADS = 32
HEAD_DIM = 128
BLOCK = 64
FRAME_BLOCKS = 32
KEEP = 32
GROUP = 4
EXP2_SCALE = HEAD_DIM ** (-0.5) * math.log2(math.e)
NT = (((1,), (1,)), ((), ()))


def norm_rows(inputs, scaling):
    widened = inputs.astype(jnp.float32)
    mean_square = jnp.mean(widened * widened, axis=-1, keepdims=True)
    return (widened * lax.rsqrt(mean_square + 1e-06) * scaling).astype(jnp.bfloat16)


def attend_tile(q_ref, k_ref, v_ref, ones_ref, o_ref, ids_ref, count, first_block, t, groups):
    null_block = v_ref.shape[0] // BLOCK - 1
    own = ids_ref[t, 0] - first_block
    key_rows, value_rows, ones_rows = [], [], []
    for slot in range(groups * GROUP):
        live = slot < count
        block = ids_ref[t, slot] - first_block
        key_rows.append(pl.ds(pl.multiple_of(jnp.where(live, block, own) * BLOCK, BLOCK), BLOCK))
        value_rows.append(
            pl.ds(pl.multiple_of(jnp.where(live, block, null_block) * BLOCK, BLOCK), BLOCK)
        )
        ones_rows.append(pl.ds(pl.multiple_of(jnp.where(live, 0, BLOCK), BLOCK), BLOCK))
    rows = pl.ds(pl.multiple_of(t * BLOCK, BLOCK), BLOCK)
    heads = [slice(h * HEAD_DIM, (h + 1) * HEAD_DIM) for h in range(2)]
    scores = []
    for lanes in heads:
        query = q_ref[rows, lanes]
        of_head = []
        for g in range(groups):
            slots = range(g * GROUP, (g + 1) * GROUP)
            keys = jnp.concatenate([k_ref[key_rows[s], lanes] for s in slots], axis=0)
            of_head.append(
                lax.dot_general(query, keys, NT, preferred_element_type=jnp.float32)
            )
        scores.append(of_head)
    for lanes, of_head in zip(heads, scores):
        peak = jnp.max(functools.reduce(jnp.maximum, of_head), axis=1, keepdims=True)
        total = jnp.zeros((BLOCK, 2 * HEAD_DIM), jnp.float32)
        for g in range(groups):
            weights = jnp.exp2((of_head[g] - peak) * EXP2_SCALE).astype(jnp.bfloat16)
            slots = range(g * GROUP, (g + 1) * GROUP)
            values = jnp.concatenate(
                [
                    jnp.concatenate([v_ref[value_rows[s], lanes], ones_ref[ones_rows[s], :]], axis=1)
                    for s in slots
                ],
                axis=0,
            )
            total = total + jnp.dot(weights, values, preferred_element_type=jnp.float32)
        o_ref[rows, lanes] = (total[:, :HEAD_DIM] / total[:, HEAD_DIM:]).astype(jnp.bfloat16)


def attend_kernel(
    ids_ref, counts_ref, first_ref, q_in, k_low, k_own, k_high, v_low, v_own, v_high,
    o_ref, q_ref, k_ref, v_ref, ones_ref, sems,
):
    frame_rows = FRAME_BLOCKS * BLOCK
    local_rows = q_in.shape[0]
    copies = []
    plan = [(q_in, q_ref.at[pl.ds(0, local_rows)])]
    for low, own, high, dest in ((k_low, k_own, k_high, k_ref), (v_low, v_own, v_high, v_ref)):
        plan.append((low, dest.at[pl.ds(0, frame_rows)]))
        plan.append((own, dest.at[pl.ds(frame_rows, local_rows)]))
        plan.append((high, dest.at[pl.ds(frame_rows + local_rows, frame_rows)]))
    for index, (source, dest) in enumerate(plan):
        copy = pltpu.make_async_copy(source, dest, sems.at[index])
        copy.start()
        copies.append(copy)
    null_row = local_rows + 2 * frame_rows
    v_ref[pl.ds(null_row, BLOCK), :] = jnp.zeros((BLOCK, v_ref.shape[1]), jnp.bfloat16)
    ones_ref[pl.ds(0, BLOCK), :] = jnp.ones((BLOCK, HEAD_DIM), jnp.bfloat16)
    ones_ref[pl.ds(BLOCK, BLOCK), :] = jnp.zeros((BLOCK, HEAD_DIM), jnp.bfloat16)
    for copy in copies:
        copy.wait()
    first_block = first_ref[0]

    def tile(t, carry):
        count = counts_ref[t]
        needed = (count + GROUP - 1) // GROUP
        for groups in range(1, KEEP // GROUP + 1):

            @pl.when(needed == groups)
            def _():
                attend_tile(
                    q_ref, k_ref, v_ref, ones_ref, o_ref, ids_ref, count, first_block, t, groups
                )

        return carry

    lax.fori_loop(0, local_rows // BLOCK, tile, 0)


def attend(keep_list, counts, first_block, query, key_parts, value_parts):
    frame_rows = FRAME_BLOCKS * BLOCK
    rows, width = query.shape
    scalar = pl.BlockSpec(memory_space=pltpu.SMEM)
    whole = pl.BlockSpec(memory_space=pl.ANY)
    reach = rows + 2 * frame_rows
    return pl.pallas_call(
        attend_kernel,
        out_shape=jax.ShapeDtypeStruct((rows, width), jnp.bfloat16),
        in_specs=[scalar] * 3 + [whole] * 7,
        out_specs=pl.BlockSpec(memory_space=pltpu.VMEM),
        scratch_shapes=[
            pltpu.VMEM((rows, width), jnp.bfloat16),
            pltpu.VMEM((reach, width), jnp.bfloat16),
            pltpu.VMEM((reach + BLOCK, width), jnp.bfloat16),
            pltpu.VMEM((2 * BLOCK, HEAD_DIM), jnp.bfloat16),
            pltpu.SemaphoreType.DMA((7,)),
        ],
        compiler_params=pltpu.CompilerParams(vmem_limit_bytes=48 * 2**20),
        cost_estimate=pl.CostEstimate(
            flops=rows * KEEP * BLOCK * width * 4,
            bytes_accessed=2 * (2 * rows + 2 * reach) * width,
            transcendentals=rows * KEEP * BLOCK * 2,
        ),
    )(keep_list, counts, first_block, query, *key_parts, *value_parts)


def with_neighbours(block):
    frame_rows = FRAME_BLOCKS * BLOCK
    count = lax.axis_size("tm")
    forward = [(i, i + 1) for i in range(count - 1)]
    backward = [(target, source) for source, target in forward]
    low = lax.ppermute(block[-frame_rows:], "tm", forward)
    high = lax.ppermute(block[:frame_rows], "tm", backward)
    return low, block, high


def to_heads(block):
    return lax.all_to_all(block, "head", split_axis=1, concat_axis=0, tiled=True)


def shards(queries, key_in, values_in, query_gain, key_gain, keep_list, counts):
    value_parts = with_neighbours(to_heads(values_in))
    key_parts = with_neighbours(to_heads(norm_rows(key_in, key_gain)))
    query = to_heads(norm_rows(queries, query_gain))
    frames_here = query.shape[0] // (FRAME_BLOCKS * BLOCK)
    first_block = (lax.axis_index("tm") * frames_here - 1) * FRAME_BLOCKS
    first_block = first_block.astype(jnp.int32).reshape(1)
    mixed_out = attend(keep_list, counts, first_block, query, key_parts, value_parts)
    return lax.all_to_all(mixed_out, "head", split_axis=0, concat_axis=1, tiled=True)


def solution(mesh):
    placed = (
        P(("tm", "head"), None),
        P(("tm", "head"), None),
        P(("tm", "head"), None),
        P(),
        P(),
        P("tm", None),
        P("tm"),
    )
    return jax.shard_map(
        shards, mesh=mesh, in_specs=placed, out_specs=P(("tm", "head"), None), check_vma=False
    )
```

```python
import functools
import math

import jax
import jax.numpy as jnp
from jax import lax
from jax.experimental import pallas as pl
from jax.experimental.pallas import tpu as pltpu
from jax.sharding import PartitionSpec as P

HEADS = 32
HEAD_DIM = 128
BLOCK = 64
FRAME_BLOCKS = 32
KEEP = 32
LINE = 4
GROUP = 4
EXP2_SCALE = HEAD_DIM ** (-0.5) * math.log2(math.e)
NT = (((1,), (1,)), ((), ()))


def attend_tile(q_ref, k_ref, v_ref, ones_ref, o_ref, slots_ref, t, groups):
    heads = [slice(h * HEAD_DIM, (h + 1) * HEAD_DIM) for h in range(2)]
    scores = []
    for lanes in heads:
        query = q_ref[t, :, lanes]
        of_head = []
        for g in range(groups):
            slots = range(g * GROUP, (g + 1) * GROUP)
            keys = jnp.concatenate([k_ref[slots_ref[t, s], :, lanes] for s in slots], axis=0)
            of_head.append(
                lax.dot_general(query, keys, NT, preferred_element_type=jnp.float32)
            )
        scores.append(of_head)
    for lanes, of_head in zip(heads, scores):
        peak = jnp.max(functools.reduce(jnp.maximum, of_head), axis=1, keepdims=True)
        total = jnp.zeros((BLOCK, 2 * HEAD_DIM), jnp.float32)
        for g in range(groups):
            weights = jnp.exp2((of_head[g] - peak) * EXP2_SCALE).astype(jnp.bfloat16)
            slots = range(g * GROUP, (g + 1) * GROUP)
            values = jnp.concatenate(
                [
                    jnp.concatenate(
                        [
                            v_ref[slots_ref[t, KEEP + s], :, lanes],
                            ones_ref[slots_ref[t, 2 * KEEP + s]],
                        ],
                        axis=1,
                    )
                    for s in slots
                ],
                axis=0,
            )
            total = total + jnp.dot(weights, values, preferred_element_type=jnp.float32)
        o_ref[t, :, lanes] = (total[:, :HEAD_DIM] / total[:, HEAD_DIM:]).astype(jnp.bfloat16)


def slot_table(keep_list, counts, first_block, null_block):
    live = jnp.arange(KEEP, dtype=jnp.int32)[None, :] < counts[:, None]
    local = keep_list - first_block
    own = FRAME_BLOCKS + jnp.arange(keep_list.shape[0], dtype=jnp.int32)[:, None]
    return jnp.concatenate(
        [
            jnp.where(live, local, own),
            jnp.where(live, local, null_block),
            jnp.where(live, 0, 1).astype(jnp.int32),
        ],
        axis=1,
    )


def norm_in_place(rows_ref, gain_ref):
    strip = 16
    strips = BLOCK // strip

    def one(index, carry):
        block = index // strips
        rows = pl.ds(pl.multiple_of(lax.rem(index, strips) * strip, strip), strip)
        widened = rows_ref[block, rows, :].astype(jnp.float32)
        mean_square = jnp.mean(widened * widened, axis=-1, keepdims=True)
        normed = widened * lax.rsqrt(mean_square + 1e-06) * gain_ref[...]
        rows_ref[block, rows, :] = normed.astype(jnp.bfloat16)
        return carry

    lax.fori_loop(0, rows_ref.shape[0] * strips, one, 0)


def whole_kernel(
    groups_n, heads_n, slots_ref, q_gain, k_gain, q_in, k_in, v_in, o_out,
    q_rows, k_rows, q_ref, k_ref, v_ref, o_ref, ones_ref,
    load_sems, own_sems, send_sems, recv_sems, halo_send, halo_recv,
    relay_ref, relay_send, relay_recv,
):
    tm = lax.axis_index("tm")
    me = lax.axis_index("head")
    part = q_in.shape[0]
    width = q_ref.shape[2]
    per_frame = FRAME_BLOCKS // part
    frames_here = part * heads_n // FRAME_BLOCKS
    V, K, Q, O = range(4)

    def part_rows(index, base=0):
        return pl.ds(base + index * part, part)

    def part_lanes(index):
        return pl.ds(pl.multiple_of(index * width, width), width)

    def partner(offset):
        return lax.rem(me + offset, heads_n)

    def exchange(which, source, dest, base, offset):
        to = partner(offset)
        return pltpu.make_async_remote_copy(
            src_ref=source.at[:, :, part_lanes(to)],
            dst_ref=dest.at[part_rows(me, base)],
            send_sem=send_sems.at[which, offset],
            recv_sem=recv_sems.at[which, offset],
            device_id=(tm, to),
            device_id_type=pl.DeviceIdType.MESH,
        )

    def give_back(offset):
        to = partner(offset)
        return pltpu.make_async_remote_copy(
            src_ref=o_ref.at[part_rows(to)],
            dst_ref=o_out.at[:, :, part_lanes(me)],
            send_sem=send_sems.at[O, offset],
            recv_sem=recv_sems.at[O, offset],
            device_id=(tm, to),
            device_id_type=pl.DeviceIdType.MESH,
        )

    def own_copy(which, source, dest, base):
        return pltpu.make_async_copy(
            source.at[:, :, part_lanes(me)], dest.at[part_rows(me, base)], own_sems.at[which]
        )

    def halo(which, buffer, chunk):
        later = chunk // per_frame
        target = tm - 1 + 2 * later
        shift = (1 - 2 * later) * frames_here * FRAME_BLOCKS
        return pltpu.make_async_remote_copy(
            src_ref=buffer.at[part_rows(chunk, FRAME_BLOCKS)],
            dst_ref=buffer.at[part_rows(chunk, FRAME_BLOCKS + shift)],
            send_sem=halo_send.at[which, chunk],
            recv_sem=halo_recv.at[which, chunk],
            device_id=(target, me),
            device_id_type=pl.DeviceIdType.MESH,
        )

    def halo_goes(chunk):
        target = tm - 1 + 2 * (chunk // per_frame)
        return jnp.logical_and(target >= 0, target < groups_n)

    def halo_comes(chunk):
        origin = tm + 1 - 2 * (chunk // per_frame)
        return jnp.logical_and(origin >= 0, origin < groups_n)

    middle = groups_n // 2
    upper = tm // middle
    is_relay = lax.rem(tm, 2) == upper
    is_middle = jnp.logical_or(tm == middle - 1, tm == middle)

    def over_relay(chunk):
        return tm + chunk // per_frame == middle

    def first_leg(which, buffer, chunk):
        later = chunk // per_frame
        x = lax.rem(chunk, 4)
        place = which * 2 + lax.rem(chunk, per_frame) // 4
        return pltpu.make_async_remote_copy(
            src_ref=buffer.at[part_rows(chunk, FRAME_BLOCKS)],
            dst_ref=relay_ref.at[place],
            send_sem=halo_send.at[which, chunk],
            recv_sem=relay_recv.at[place],
            device_id=((1 - later) * (middle + 1) + 2 * x, me),
            device_id_type=pl.DeviceIdType.MESH,
        )

    def second_leg(which, buffer, index):
        later = 1 - upper
        place = which * 2 + index
        chunk = later * per_frame + index * 4 + lax.rem(tm, middle) // 2
        shift = (1 - 2 * later) * frames_here * FRAME_BLOCKS
        return pltpu.make_async_remote_copy(
            src_ref=relay_ref.at[place],
            dst_ref=buffer.at[part_rows(chunk, FRAME_BLOCKS + shift)],
            send_sem=relay_send.at[place],
            recv_sem=halo_recv.at[which, chunk],
            device_id=(middle - 1 + later, me),
            device_id_type=pl.DeviceIdType.MESH,
        )

    def relay(which, buffer):
        @pl.when(is_relay)
        def _():
            for index in range(2):
                first_leg(which, buffer, index * 4).wait_recv()
                second_leg(which, buffer, index).start()

    def send_halo(which, buffer, chunk):
        @pl.when(jnp.logical_and(halo_goes(chunk), jnp.logical_not(over_relay(chunk))))
        def _():
            halo(which, buffer, chunk).start()

        @pl.when(over_relay(chunk))
        def _():
            first_leg(which, buffer, chunk).start()

    k_load = pltpu.make_async_copy(k_in, k_rows, load_sems.at[0])
    q_load = pltpu.make_async_copy(q_in, q_rows, load_sems.at[1])
    k_load.start()
    q_load.start()

    barrier = pltpu.get_barrier_semaphore()
    for offset in range(1, heads_n):
        pl.semaphore_signal(
            barrier, inc=1, device_id=(tm, partner(offset)), device_id_type=pl.DeviceIdType.MESH
        )

    @pl.when(tm > 0)
    def _():
        pl.semaphore_signal(
            barrier, inc=1, device_id=(tm - 1, me), device_id_type=pl.DeviceIdType.MESH
        )

    @pl.when(tm < groups_n - 1)
    def _():
        pl.semaphore_signal(
            barrier, inc=1, device_id=(tm + 1, me), device_id_type=pl.DeviceIdType.MESH
        )

    @pl.when(is_relay)
    def _():
        for other in (middle - 1, middle):
            pl.semaphore_signal(
                barrier, inc=1, device_id=(other, me), device_id_type=pl.DeviceIdType.MESH
            )

    @pl.when(is_middle)
    def _():
        for x in range(4):
            for other in (2 * x, middle + 1 + 2 * x):
                pl.semaphore_signal(
                    barrier, inc=1, device_id=(other, me), device_id_type=pl.DeviceIdType.MESH
                )

    expected = heads_n - 1 + (tm > 0).astype(jnp.int32) + (tm < groups_n - 1).astype(jnp.int32)
    expected += 2 * is_relay.astype(jnp.int32) + 8 * is_middle.astype(jnp.int32)
    pl.semaphore_wait(barrier, expected)

    def each_chunk(body):
        def step(chunk, carry):
            body(chunk)
            return carry

        lax.fori_loop(0, heads_n, step, 0)

    line, lane_z = me // LINE, lax.rem(me, LINE)
    near, half = lax.rem((lane_z + 1) // 2, 2), lane_z // 2

    def each_target(body):
        def one(slot):
            crosses = 1 - lax.rem(slot // 8 + near, 2)
            ahead, other = lax.rem(slot, 8) // 2, lax.rem(slot, 2)
            z = lax.rem(half + crosses, 2) * 2 + lax.rem(lane_z + other, 2)
            to = lax.rem(line + ahead, heads_n // LINE) * LINE + z

            @pl.when(to != me)
            def _():
                body(lax.rem(to - me + heads_n, heads_n))

        each_chunk(one)

    def each_source(body):
        def one(slot):
            behind, same = lax.rem(slot, 8) // 2, lax.rem(slot, 2)
            side = lax.rem(half + 1 - same, 2)
            inner = lax.rem(same + slot // 8, 2)
            z = side * 3 + inner * (1 - 2 * side)
            source = lax.rem(line + heads_n // LINE - behind, heads_n // LINE) * LINE + z

            @pl.when(source != me)
            def _():
                body(lax.rem(me - source + heads_n, heads_n))

        each_chunk(one)

    v_args = (V, v_in, v_ref, FRAME_BLOCKS)
    k_args = (K, k_rows, k_ref, FRAME_BLOCKS)
    q_args = (Q, q_rows, q_ref, 0)
    each_target(lambda offset: exchange(*v_args, offset).start())
    v_own = own_copy(*v_args)
    v_own.start()
    k_load.wait()
    norm_in_place(k_rows, k_gain)
    each_target(lambda offset: exchange(*k_args, offset).start())
    k_own = own_copy(*k_args)
    k_own.start()
    q_load.wait()
    norm_in_place(q_rows, q_gain)
    q_own = own_copy(*q_args)
    q_own.start()
    v_ref[v_ref.shape[0] - 1] = jnp.zeros((BLOCK, width), jnp.bfloat16)
    ones_ref[0] = jnp.ones((BLOCK, HEAD_DIM), jnp.bfloat16)
    ones_ref[1] = jnp.zeros((BLOCK, HEAD_DIM), jnp.bfloat16)

    v_own.wait()
    send_halo(V, v_ref, me)

    def take_v(offset):
        exchange(*v_args, offset).wait_recv()
        send_halo(V, v_ref, lax.rem(me + heads_n - offset, heads_n))

    each_source(take_v)
    each_target(lambda offset: exchange(*q_args, offset).start())
    k_own.wait()
    send_halo(K, k_ref, me)

    def take_k(offset):
        exchange(*k_args, offset).wait_recv()
        send_halo(K, k_ref, lax.rem(me + heads_n - offset, heads_n))

    each_source(take_k)
    relay(V, v_ref)
    relay(K, k_ref)

    def take_halo(chunk):
        @pl.when(halo_comes(chunk))
        def _():
            halo(V, v_ref, chunk).wait_recv()
            halo(K, k_ref, chunk).wait_recv()

    each_chunk(take_halo)
    q_own.wait()
    def attend_part(source):
        def tile(index, carry):
            t = source * part + index
            attend_tile(q_ref, k_ref, v_ref, ones_ref, o_ref, slots_ref, t, KEEP // GROUP)
            return carry

        lax.fori_loop(0, part, tile, 0)

    attend_part(me)
    o_own = pltpu.make_async_copy(
        o_ref.at[part_rows(me)], o_out.at[:, :, part_lanes(me)], own_sems.at[O]
    )
    o_own.start()

    def serve(offset):
        exchange(*q_args, offset).wait_recv()
        attend_part(lax.rem(me + heads_n - offset, heads_n))
        give_back(heads_n - offset).start()

    each_source(serve)

    def finish(offset):
        for args in (v_args, k_args, q_args):
            exchange(*args, offset).wait_send()
        give_back(offset).wait_send()

    each_target(finish)

    def finish_halo(chunk):
        @pl.when(halo_goes(chunk))
        def _():
            halo(V, v_ref, chunk).wait_send()
            halo(K, k_ref, chunk).wait_send()

    each_chunk(finish_halo)
    @pl.when(is_relay)
    def _():
        for which, buffer in ((V, v_ref), (K, k_ref)):
            for index in range(2):
                second_leg(which, buffer, index).wait_send()

    o_own.wait()
    each_target(lambda offset: give_back(offset).wait_recv())


def shards(queries, key_in, values_in, query_gain, key_gain, keep_list, counts):
    groups_n, heads_n = lax.axis_size("tm"), lax.axis_size("head")
    rows, features = queries.shape
    part = rows // BLOCK
    width = features // heads_n
    local_blocks = part * heads_n
    reach = local_blocks + 2 * FRAME_BLOCKS
    first_block = lax.axis_index("tm") * local_blocks - FRAME_BLOCKS
    slots = slot_table(keep_list, counts, first_block, reach)
    scalar = pl.BlockSpec(memory_space=pltpu.SMEM)
    vector = pl.BlockSpec(memory_space=pltpu.VMEM)
    whole = pl.BlockSpec(memory_space=pl.ANY)
    dma = pltpu.SemaphoreType.DMA
    blocks = (part, BLOCK, features)
    bf16 = jnp.bfloat16
    attended = pl.pallas_call(
        functools.partial(whole_kernel, groups_n, heads_n),
        out_shape=jax.ShapeDtypeStruct(blocks, bf16),
        in_specs=[scalar] + [vector] * 2 + [whole] * 3,
        out_specs=whole,
        scratch_shapes=[
            pltpu.VMEM(blocks, bf16),
            pltpu.VMEM(blocks, bf16),
            pltpu.VMEM((local_blocks, BLOCK, width), bf16),
            pltpu.VMEM((reach, BLOCK, width), bf16),
            pltpu.VMEM((reach + 1, BLOCK, width), bf16),
            pltpu.VMEM((local_blocks, BLOCK, width), bf16),
            pltpu.VMEM((2, BLOCK, HEAD_DIM), bf16),
            dma((2,)),
            dma((4,)),
            dma((4, heads_n)),
            dma((4, heads_n)),
            dma((2, heads_n)),
            dma((2, heads_n)),
            pltpu.VMEM((4, part, BLOCK, width), bf16),
            dma((4,)),
            dma((4,)),
        ],
        compiler_params=pltpu.CompilerParams(
            collective_id=0, has_side_effects=True, vmem_limit_bytes=48 * 2**20
        ),
        cost_estimate=pl.CostEstimate(
            flops=local_blocks * BLOCK * KEEP * BLOCK * width * 4,
            bytes_accessed=8 * rows * features,
            transcendentals=local_blocks * BLOCK * KEEP * BLOCK * 2,
        ),
    )(
        slots, query_gain.reshape(1, -1), key_gain.reshape(1, -1),
        queries.reshape(blocks), key_in.reshape(blocks), values_in.reshape(blocks),
    )
    return attended.reshape(rows, features)


def solution(mesh):
    placed = (
        P(("tm", "head"), None),
        P(("tm", "head"), None),
        P(("tm", "head"), None),
        P(),
        P(),
        P("tm", None),
        P("tm"),
    )
    return jax.shard_map(
        shards, mesh=mesh, in_specs=placed, out_specs=P(("tm", "head"), None), check_vma=False
    )
```

```python
import functools
import math

import jax
import jax.numpy as jnp
from jax import lax
from jax.experimental import pallas as pl
from jax.experimental.pallas import tpu as pltpu
from jax.sharding import PartitionSpec as P

HEADS = 32
HEAD_DIM = 128
BLOCK = 64
FRAME_BLOCKS = 32
KEEP = 32
PAIR = 2
LINE = 4
GROUP = 4
EXP2_SCALE = HEAD_DIM ** (-0.5) * math.log2(math.e)
NT = (((1,), (1,)), ((), ()))


def attend_tile(q_ref, k_ref, v_ref, ones_ref, o_ref, slots_ref, t, groups):
    heads = [slice(h * HEAD_DIM, (h + 1) * HEAD_DIM) for h in range(2)]
    scores = []
    for lanes in heads:
        query = q_ref[t, :, lanes]
        of_head = []
        for g in range(groups):
            slots = range(g * GROUP, (g + 1) * GROUP)
            keys = jnp.concatenate([k_ref[slots_ref[t, s], :, lanes] for s in slots], axis=0)
            of_head.append(
                lax.dot_general(query, keys, NT, preferred_element_type=jnp.float32)
            )
        scores.append(of_head)
    for lanes, of_head in zip(heads, scores):
        peak = jnp.max(functools.reduce(jnp.maximum, of_head), axis=1, keepdims=True)
        total = jnp.zeros((BLOCK, 2 * HEAD_DIM), jnp.float32)
        for g in range(groups):
            weights = jnp.exp2((of_head[g] - peak) * EXP2_SCALE).astype(jnp.bfloat16)
            slots = range(g * GROUP, (g + 1) * GROUP)
            values = jnp.concatenate(
                [
                    jnp.concatenate(
                        [
                            v_ref[slots_ref[t, KEEP + s], :, lanes],
                            ones_ref[slots_ref[t, 2 * KEEP + s]],
                        ],
                        axis=1,
                    )
                    for s in slots
                ],
                axis=0,
            )
            total = total + jnp.dot(weights, values, preferred_element_type=jnp.float32)
        o_ref[t, :, lanes] = (total[:, :HEAD_DIM] / total[:, HEAD_DIM:]).astype(jnp.bfloat16)


def slot_table(keep_list, counts, first_block, null_block):
    live = jnp.arange(KEEP, dtype=jnp.int32)[None, :] < counts[:, None]
    local = keep_list - first_block
    own = FRAME_BLOCKS + jnp.arange(keep_list.shape[0], dtype=jnp.int32)[:, None]
    return jnp.concatenate(
        [
            jnp.where(live, local, own),
            jnp.where(live, local, null_block),
            jnp.where(live, 0, 1).astype(jnp.int32),
        ],
        axis=1,
    )


def norm_in_place(rows_ref, gain_ref):
    strip = 16
    strips = BLOCK // strip

    def one(index, carry):
        block = index // strips
        rows = pl.ds(pl.multiple_of(lax.rem(index, strips) * strip, strip), strip)
        widened = rows_ref[block, rows, :].astype(jnp.float32)
        mean_square = jnp.mean(widened * widened, axis=-1, keepdims=True)
        normed = widened * lax.rsqrt(mean_square + 1e-06) * gain_ref[...]
        rows_ref[block, rows, :] = normed.astype(jnp.bfloat16)
        return carry

    lax.fori_loop(0, rows_ref.shape[0] * strips, one, 0)


def whole_kernel(
    groups_n, heads_n, slots_ref, q_gain, k_gain, q_in, k_in, v_in, o_out,
    q_rows, k_rows, q_ref, k_ref, v_ref, o_ref, ones_ref,
    load_sems, own_sems, send_sems, recv_sems, halo_send, halo_recv,
    relay_ref, relay_send, relay_recv,
):
    tm = lax.axis_index("tm")
    me = lax.axis_index("head")
    part = q_in.shape[0]
    width = q_ref.shape[2]
    per_frame = FRAME_BLOCKS // part
    frames_here = part * heads_n // FRAME_BLOCKS
    V, K, Q, O = range(4)

    def part_rows(index, base=0):
        return pl.ds(base + index * part, part)

    def part_lanes(index):
        return pl.ds(pl.multiple_of(index * width, width), width)

    def partner(offset):
        return lax.rem(me + offset, heads_n)

    def exchange(which, source, dest, base, offset):
        to = partner(offset)
        return pltpu.make_async_remote_copy(
            src_ref=source.at[:, :, part_lanes(to)],
            dst_ref=dest.at[part_rows(me, base)],
            send_sem=send_sems.at[which, offset],
            recv_sem=recv_sems.at[which, offset],
            device_id=(tm, to),
            device_id_type=pl.DeviceIdType.MESH,
        )

    def give_back(offset):
        to = partner(offset)
        return pltpu.make_async_remote_copy(
            src_ref=o_ref.at[part_rows(to)],
            dst_ref=o_out.at[:, :, part_lanes(me)],
            send_sem=send_sems.at[O, offset],
            recv_sem=recv_sems.at[O, offset],
            device_id=(tm, to),
            device_id_type=pl.DeviceIdType.MESH,
        )

    def own_copy(which, source, dest, base):
        return pltpu.make_async_copy(
            source.at[:, :, part_lanes(me)], dest.at[part_rows(me, base)], own_sems.at[which]
        )

    def halo(which, buffer, chunk):
        later = chunk // per_frame
        target = tm - 1 + 2 * later
        shift = (1 - 2 * later) * frames_here * FRAME_BLOCKS
        return pltpu.make_async_remote_copy(
            src_ref=buffer.at[part_rows(chunk, FRAME_BLOCKS)],
            dst_ref=buffer.at[part_rows(chunk, FRAME_BLOCKS + shift)],
            send_sem=halo_send.at[which, chunk],
            recv_sem=halo_recv.at[which, chunk],
            device_id=(target, me),
            device_id_type=pl.DeviceIdType.MESH,
        )

    def halo_goes(chunk):
        target = tm - 1 + 2 * (chunk // per_frame)
        return jnp.logical_and(target >= 0, target < groups_n)

    def halo_comes(chunk):
        origin = tm + 1 - 2 * (chunk // per_frame)
        return jnp.logical_and(origin >= 0, origin < groups_n)

    middle = groups_n // 2
    upper = tm // middle
    is_relay = lax.rem(tm, 2) == upper
    is_middle = jnp.logical_or(tm == middle - 1, tm == middle)

    def over_relay(chunk):
        return tm + chunk // per_frame == middle

    def first_leg(which, buffer, chunk):
        later = chunk // per_frame
        x = lax.rem(chunk, 4)
        place = which * 2 + lax.rem(chunk, per_frame) // 4
        return pltpu.make_async_remote_copy(
            src_ref=buffer.at[part_rows(chunk, FRAME_BLOCKS)],
            dst_ref=relay_ref.at[place],
            send_sem=halo_send.at[which, chunk],
            recv_sem=relay_recv.at[place],
            device_id=((1 - later) * (middle + 1) + 2 * x, me),
            device_id_type=pl.DeviceIdType.MESH,
        )

    def second_leg(which, buffer, index):
        later = 1 - upper
        place = which * 2 + index
        chunk = later * per_frame + index * 4 + lax.rem(tm, middle) // 2
        shift = (1 - 2 * later) * frames_here * FRAME_BLOCKS
        return pltpu.make_async_remote_copy(
            src_ref=relay_ref.at[place],
            dst_ref=buffer.at[part_rows(chunk, FRAME_BLOCKS + shift)],
            send_sem=relay_send.at[place],
            recv_sem=halo_recv.at[which, chunk],
            device_id=(middle - 1 + later, me),
            device_id_type=pl.DeviceIdType.MESH,
        )

    def relay(which, buffer):
        @pl.when(is_relay)
        def _():
            for index in range(2):
                first_leg(which, buffer, index * 4).wait_recv()
                second_leg(which, buffer, index).start()

    def send_halo(which, buffer, chunk):
        @pl.when(jnp.logical_and(halo_goes(chunk), jnp.logical_not(over_relay(chunk))))
        def _():
            halo(which, buffer, chunk).start()

        @pl.when(over_relay(chunk))
        def _():
            first_leg(which, buffer, chunk).start()

    k_load = pltpu.make_async_copy(k_in, k_rows, load_sems.at[0])
    q_load = pltpu.make_async_copy(q_in, q_rows, load_sems.at[1])
    k_load.start()
    q_load.start()

    barrier = pltpu.get_barrier_semaphore()
    for offset in range(1, heads_n):
        pl.semaphore_signal(
            barrier, inc=1, device_id=(tm, partner(offset)), device_id_type=pl.DeviceIdType.MESH
        )

    @pl.when(tm > 0)
    def _():
        pl.semaphore_signal(
            barrier, inc=1, device_id=(tm - 1, me), device_id_type=pl.DeviceIdType.MESH
        )

    @pl.when(tm < groups_n - 1)
    def _():
        pl.semaphore_signal(
            barrier, inc=1, device_id=(tm + 1, me), device_id_type=pl.DeviceIdType.MESH
        )

    @pl.when(is_relay)
    def _():
        for other in (middle - 1, middle):
            pl.semaphore_signal(
                barrier, inc=1, device_id=(other, me), device_id_type=pl.DeviceIdType.MESH
            )

    @pl.when(is_middle)
    def _():
        for x in range(4):
            for other in (2 * x, middle + 1 + 2 * x):
                pl.semaphore_signal(
                    barrier, inc=1, device_id=(other, me), device_id_type=pl.DeviceIdType.MESH
                )

    expected = heads_n - 1 + (tm > 0).astype(jnp.int32) + (tm < groups_n - 1).astype(jnp.int32)
    expected += 2 * is_relay.astype(jnp.int32) + 8 * is_middle.astype(jnp.int32)
    pl.semaphore_wait(barrier, expected)

    def each_chunk(body):
        def step(chunk, carry):
            body(chunk)
            return carry

        lax.fori_loop(0, heads_n, step, 0)

    line, lane_z = me // LINE, lax.rem(me, LINE)
    near, half = lax.rem((lane_z + 1) // 2, 2), lane_z // 2

    def each_target(body):
        def one(slot):
            crosses = 1 - lax.rem(slot // 8 + near, 2)
            ahead, other = lax.rem(slot, 8) // 2, lax.rem(slot, 2)
            z = lax.rem(half + crosses, 2) * 2 + lax.rem(lane_z + other, 2)
            to = lax.rem(me + slot, heads_n)

            @pl.when(to != me)
            def _():
                body(lax.rem(to - me + heads_n, heads_n))

        each_chunk(one)

    def each_source(body):
        def one(slot):
            behind, same = lax.rem(slot, 8) // 2, lax.rem(slot, 2)
            side = lax.rem(half + 1 - same, 2)
            inner = lax.rem(same + slot // 8, 2)
            z = side * 3 + inner * (1 - 2 * side)
            source = lax.rem(me + heads_n - slot, heads_n)

            @pl.when(source != me)
            def _():
                body(lax.rem(me - source + heads_n, heads_n))

        each_chunk(one)

    v_args = (V, v_in, v_ref, FRAME_BLOCKS)
    k_args = (K, k_rows, k_ref, FRAME_BLOCKS)
    q_args = (Q, q_rows, q_ref, 0)
    each_target(lambda offset: exchange(*v_args, offset).start())
    v_own = own_copy(*v_args)
    v_own.start()
    k_load.wait()
    norm_in_place(k_rows, k_gain)
    each_target(lambda offset: exchange(*k_args, offset).start())
    k_own = own_copy(*k_args)
    k_own.start()
    q_load.wait()
    norm_in_place(q_rows, q_gain)
    q_own = own_copy(*q_args)
    q_own.start()
    v_ref[v_ref.shape[0] - 1] = jnp.zeros((BLOCK, width), jnp.bfloat16)
    ones_ref[0] = jnp.ones((BLOCK, HEAD_DIM), jnp.bfloat16)
    ones_ref[1] = jnp.zeros((BLOCK, HEAD_DIM), jnp.bfloat16)

    v_own.wait()
    send_halo(V, v_ref, me)

    def take_v(offset):
        exchange(*v_args, offset).wait_recv()
        send_halo(V, v_ref, lax.rem(me + heads_n - offset, heads_n))

    each_source(take_v)
    k_own.wait()
    send_halo(K, k_ref, me)

    def take_k(offset):
        exchange(*k_args, offset).wait_recv()
        send_halo(K, k_ref, lax.rem(me + heads_n - offset, heads_n))

    relay(V, v_ref)
    each_source(take_k)
    relay(K, k_ref)
    each_target(lambda offset: exchange(*q_args, offset).start())

    def take_halo(chunk):
        @pl.when(halo_comes(chunk))
        def _():
            halo(V, v_ref, chunk).wait_recv()
            halo(K, k_ref, chunk).wait_recv()

    each_chunk(take_halo)
    q_own.wait()
    def attend_part(source):
        def tile(index, carry):
            for more in range(PAIR):
                t = source * part + index * PAIR + more
                attend_tile(q_ref, k_ref, v_ref, ones_ref, o_ref, slots_ref, t, KEEP // GROUP)
            return carry

        lax.fori_loop(0, part // PAIR, tile, 0)

    attend_part(me)
    o_own = pltpu.make_async_copy(
        o_ref.at[part_rows(me)], o_out.at[:, :, part_lanes(me)], own_sems.at[O]
    )
    o_own.start()

    def serve(offset):
        exchange(*q_args, offset).wait_recv()
        attend_part(lax.rem(me + heads_n - offset, heads_n))
        give_back(heads_n - offset).start()

    each_source(serve)

    def finish(offset):
        for args in (v_args, k_args, q_args):
            exchange(*args, offset).wait_send()
        give_back(offset).wait_send()

    each_target(finish)

    def finish_halo(chunk):
        @pl.when(halo_goes(chunk))
        def _():
            halo(V, v_ref, chunk).wait_send()
            halo(K, k_ref, chunk).wait_send()

    each_chunk(finish_halo)
    @pl.when(is_relay)
    def _():
        for which, buffer in ((V, v_ref), (K, k_ref)):
            for index in range(2):
                second_leg(which, buffer, index).wait_send()

    o_own.wait()
    each_target(lambda offset: give_back(offset).wait_recv())


def shards(queries, key_in, values_in, query_gain, key_gain, keep_list, counts):
    groups_n, heads_n = lax.axis_size("tm"), lax.axis_size("head")
    rows, features = queries.shape
    part = rows // BLOCK
    width = features // heads_n
    local_blocks = part * heads_n
    reach = local_blocks + 2 * FRAME_BLOCKS
    first_block = lax.axis_index("tm") * local_blocks - FRAME_BLOCKS
    slots = slot_table(keep_list, counts, first_block, reach)
    scalar = pl.BlockSpec(memory_space=pltpu.SMEM)
    vector = pl.BlockSpec(memory_space=pltpu.VMEM)
    whole = pl.BlockSpec(memory_space=pl.ANY)
    dma = pltpu.SemaphoreType.DMA
    blocks = (part, BLOCK, features)
    bf16 = jnp.bfloat16
    attended = pl.pallas_call(
        functools.partial(whole_kernel, groups_n, heads_n),
        out_shape=jax.ShapeDtypeStruct(blocks, bf16),
        in_specs=[scalar] + [vector] * 2 + [whole] * 3,
        out_specs=whole,
        scratch_shapes=[
            pltpu.VMEM(blocks, bf16),
            pltpu.VMEM(blocks, bf16),
            pltpu.VMEM((local_blocks, BLOCK, width), bf16),
            pltpu.VMEM((reach, BLOCK, width), bf16),
            pltpu.VMEM((reach + 1, BLOCK, width), bf16),
            pltpu.VMEM((local_blocks, BLOCK, width), bf16),
            pltpu.VMEM((2, BLOCK, HEAD_DIM), bf16),
            dma((2,)),
            dma((4,)),
            dma((4, heads_n)),
            dma((4, heads_n)),
            dma((2, heads_n)),
            dma((2, heads_n)),
            pltpu.VMEM((4, part, BLOCK, width), bf16),
            dma((4,)),
            dma((4,)),
        ],
        compiler_params=pltpu.CompilerParams(
            collective_id=0, has_side_effects=True, vmem_limit_bytes=48 * 2**20
        ),
        cost_estimate=pl.CostEstimate(
            flops=local_blocks * BLOCK * KEEP * BLOCK * width * 4,
            bytes_accessed=8 * rows * features,
            transcendentals=local_blocks * BLOCK * KEEP * BLOCK * 2,
        ),
    )(
        slots, query_gain.reshape(1, -1), key_gain.reshape(1, -1),
        queries.reshape(blocks), key_in.reshape(blocks), values_in.reshape(blocks),
    )
    return attended.reshape(rows, features)


def solution(mesh):
    placed = (
        P(("tm", "head"), None),
        P(("tm", "head"), None),
        P(("tm", "head"), None),
        P(),
        P(),
        P("tm", None),
        P("tm"),
    )
    return jax.shard_map(
        shards, mesh=mesh, in_specs=placed, out_specs=P(("tm", "head"), None), check_vma=False
    )
```

```python
import functools
import math

import jax
import jax.numpy as jnp
from jax import lax
from jax.experimental import pallas as pl
from jax.experimental.pallas import tpu as pltpu
from jax.sharding import PartitionSpec as P

HEADS = 32
HEAD_DIM = 128
BLOCK = 64
FRAME_BLOCKS = 32
KEEP = 32
PAIR = 4
LINE = 4
GROUP = 4
EXP2_SCALE = HEAD_DIM ** (-0.5) * math.log2(math.e)
NT = (((1,), (1,)), ((), ()))


def attend_tile(q_ref, k_ref, v_ref, ones_ref, o_ref, slots_ref, t, groups):
    heads = [slice(h * HEAD_DIM, (h + 1) * HEAD_DIM) for h in range(2)]
    scores = []
    for lanes in heads:
        query = q_ref[t, :, lanes]
        of_head = []
        for g in range(groups):
            slots = range(g * GROUP, (g + 1) * GROUP)
            keys = jnp.concatenate([k_ref[slots_ref[t, s], :, lanes] for s in slots], axis=0)
            of_head.append(
                lax.dot_general(query, keys, NT, preferred_element_type=jnp.float32)
            )
        scores.append(of_head)
    for lanes, of_head in zip(heads, scores):
        peak = jnp.max(functools.reduce(jnp.maximum, of_head), axis=1, keepdims=True)
        total = jnp.zeros((BLOCK, 2 * HEAD_DIM), jnp.float32)
        for g in range(groups):
            weights = jnp.exp2((of_head[g] - peak) * EXP2_SCALE).astype(jnp.bfloat16)
            slots = range(g * GROUP, (g + 1) * GROUP)
            values = jnp.concatenate(
                [
                    jnp.concatenate(
                        [
                            v_ref[slots_ref[t, KEEP + s], :, lanes],
                            ones_ref[slots_ref[t, 2 * KEEP + s]],
                        ],
                        axis=1,
                    )
                    for s in slots
                ],
                axis=0,
            )
            total = total + jnp.dot(weights, values, preferred_element_type=jnp.float32)
        o_ref[t, :, lanes] = (total[:, :HEAD_DIM] / total[:, HEAD_DIM:]).astype(jnp.bfloat16)


def slot_table(keep_list, counts, first_block, null_block):
    live = jnp.arange(KEEP, dtype=jnp.int32)[None, :] < counts[:, None]
    local = keep_list - first_block
    own = FRAME_BLOCKS + jnp.arange(keep_list.shape[0], dtype=jnp.int32)[:, None]
    return jnp.concatenate(
        [
            jnp.where(live, local, own),
            jnp.where(live, local, null_block),
            jnp.where(live, 0, 1).astype(jnp.int32),
        ],
        axis=1,
    )


def norm_in_place(rows_ref, gain_ref):
    strip = 16
    strips = BLOCK // strip

    def one(index, carry):
        block = index // strips
        rows = pl.ds(pl.multiple_of(lax.rem(index, strips) * strip, strip), strip)
        widened = rows_ref[block, rows, :].astype(jnp.float32)
        mean_square = jnp.mean(widened * widened, axis=-1, keepdims=True)
        normed = widened * lax.rsqrt(mean_square + 1e-06) * gain_ref[...]
        rows_ref[block, rows, :] = normed.astype(jnp.bfloat16)
        return carry

    lax.fori_loop(0, rows_ref.shape[0] * strips, one, 0)


def whole_kernel(
    groups_n, heads_n, slots_ref, q_gain, k_gain, q_in, k_in, v_in, o_out,
    q_rows, k_rows, q_ref, k_ref, v_ref, o_ref, ones_ref,
    load_sems, own_sems, send_sems, recv_sems, halo_send, halo_recv,
    relay_ref, relay_send, relay_recv,
):
    tm = lax.axis_index("tm")
    me = lax.axis_index("head")
    part = q_in.shape[0]
    width = q_ref.shape[2]
    per_frame = FRAME_BLOCKS // part
    frames_here = part * heads_n // FRAME_BLOCKS
    V, K, Q, O = range(4)

    def part_rows(index, base=0):
        return pl.ds(base + index * part, part)

    def part_lanes(index):
        return pl.ds(pl.multiple_of(index * width, width), width)

    def partner(offset):
        return lax.rem(me + offset, heads_n)

    def exchange(which, source, dest, base, offset):
        to = partner(offset)
        return pltpu.make_async_remote_copy(
            src_ref=source.at[:, :, part_lanes(to)],
            dst_ref=dest.at[part_rows(me, base)],
            send_sem=send_sems.at[which, offset],
            recv_sem=recv_sems.at[which, offset],
            device_id=(tm, to),
            device_id_type=pl.DeviceIdType.MESH,
        )

    def give_back(offset):
        to = partner(offset)
        return pltpu.make_async_remote_copy(
            src_ref=o_ref.at[part_rows(to)],
            dst_ref=o_out.at[:, :, part_lanes(me)],
            send_sem=send_sems.at[O, offset],
            recv_sem=recv_sems.at[O, offset],
            device_id=(tm, to),
            device_id_type=pl.DeviceIdType.MESH,
        )

    def own_copy(which, source, dest, base):
        return pltpu.make_async_copy(
            source.at[:, :, part_lanes(me)], dest.at[part_rows(me, base)], own_sems.at[which]
        )

    def halo(which, buffer, chunk):
        later = chunk // per_frame
        target = tm - 1 + 2 * later
        shift = (1 - 2 * later) * frames_here * FRAME_BLOCKS
        return pltpu.make_async_remote_copy(
            src_ref=buffer.at[part_rows(chunk, FRAME_BLOCKS)],
            dst_ref=buffer.at[part_rows(chunk, FRAME_BLOCKS + shift)],
            send_sem=halo_send.at[which, chunk],
            recv_sem=halo_recv.at[which, chunk],
            device_id=(target, me),
            device_id_type=pl.DeviceIdType.MESH,
        )

    def halo_goes(chunk):
        target = tm - 1 + 2 * (chunk // per_frame)
        return jnp.logical_and(target >= 0, target < groups_n)

    def halo_comes(chunk):
        origin = tm + 1 - 2 * (chunk // per_frame)
        return jnp.logical_and(origin >= 0, origin < groups_n)

    middle = groups_n // 2
    upper = tm // middle
    is_relay = lax.rem(tm, 2) == upper
    is_middle = jnp.logical_or(tm == middle - 1, tm == middle)

    def over_relay(chunk):
        return tm + chunk // per_frame == middle

    def first_leg(which, buffer, chunk):
        later = chunk // per_frame
        x = lax.rem(chunk, 4)
        place = which * 2 + lax.rem(chunk, per_frame) // 4
        return pltpu.make_async_remote_copy(
            src_ref=buffer.at[part_rows(chunk, FRAME_BLOCKS)],
            dst_ref=relay_ref.at[place],
            send_sem=halo_send.at[which, chunk],
            recv_sem=relay_recv.at[place],
            device_id=((1 - later) * (middle + 1) + 2 * x, me),
            device_id_type=pl.DeviceIdType.MESH,
        )

    def second_leg(which, buffer, index):
        later = 1 - upper
        place = which * 2 + index
        chunk = later * per_frame + index * 4 + lax.rem(tm, middle) // 2
        shift = (1 - 2 * later) * frames_here * FRAME_BLOCKS
        return pltpu.make_async_remote_copy(
            src_ref=relay_ref.at[place],
            dst_ref=buffer.at[part_rows(chunk, FRAME_BLOCKS + shift)],
            send_sem=relay_send.at[place],
            recv_sem=halo_recv.at[which, chunk],
            device_id=(middle - 1 + later, me),
            device_id_type=pl.DeviceIdType.MESH,
        )

    def relay(which, buffer):
        @pl.when(is_relay)
        def _():
            for index in range(2):
                first_leg(which, buffer, index * 4).wait_recv()
                second_leg(which, buffer, index).start()

    def send_halo(which, buffer, chunk):
        @pl.when(jnp.logical_and(halo_goes(chunk), jnp.logical_not(over_relay(chunk))))
        def _():
            halo(which, buffer, chunk).start()

        @pl.when(over_relay(chunk))
        def _():
            first_leg(which, buffer, chunk).start()

    k_load = pltpu.make_async_copy(k_in, k_rows, load_sems.at[0])
    q_load = pltpu.make_async_copy(q_in, q_rows, load_sems.at[1])
    k_load.start()
    q_load.start()

    barrier = pltpu.get_barrier_semaphore()
    for offset in range(1, heads_n):
        pl.semaphore_signal(
            barrier, inc=1, device_id=(tm, partner(offset)), device_id_type=pl.DeviceIdType.MESH
        )

    @pl.when(tm > 0)
    def _():
        pl.semaphore_signal(
            barrier, inc=1, device_id=(tm - 1, me), device_id_type=pl.DeviceIdType.MESH
        )

    @pl.when(tm < groups_n - 1)
    def _():
        pl.semaphore_signal(
            barrier, inc=1, device_id=(tm + 1, me), device_id_type=pl.DeviceIdType.MESH
        )

    @pl.when(is_relay)
    def _():
        for other in (middle - 1, middle):
            pl.semaphore_signal(
                barrier, inc=1, device_id=(other, me), device_id_type=pl.DeviceIdType.MESH
            )

    @pl.when(is_middle)
    def _():
        for x in range(4):
            for other in (2 * x, middle + 1 + 2 * x):
                pl.semaphore_signal(
                    barrier, inc=1, device_id=(other, me), device_id_type=pl.DeviceIdType.MESH
                )

    expected = heads_n - 1 + (tm > 0).astype(jnp.int32) + (tm < groups_n - 1).astype(jnp.int32)
    expected += 2 * is_relay.astype(jnp.int32) + 8 * is_middle.astype(jnp.int32)
    pl.semaphore_wait(barrier, expected)

    def each_chunk(body):
        def step(chunk, carry):
            body(chunk)
            return carry

        lax.fori_loop(0, heads_n, step, 0)

    line, lane_z = me // LINE, lax.rem(me, LINE)
    near, half = lax.rem((lane_z + 1) // 2, 2), lane_z // 2

    def each_target(body):
        def one(slot):
            crosses = 1 - lax.rem(slot // 8 + near, 2)
            ahead, other = lax.rem(slot, 8) // 2, lax.rem(slot, 2)
            z = lax.rem(half + crosses, 2) * 2 + lax.rem(lane_z + other, 2)
            to = lax.rem(me + slot, heads_n)

            @pl.when(to != me)
            def _():
                body(lax.rem(to - me + heads_n, heads_n))

        each_chunk(one)

    def each_source(body):
        def one(slot):
            behind, same = lax.rem(slot, 8) // 2, lax.rem(slot, 2)
            side = lax.rem(half + 1 - same, 2)
            inner = lax.rem(same + slot // 8, 2)
            z = side * 3 + inner * (1 - 2 * side)
            source = lax.rem(me + heads_n - slot, heads_n)

            @pl.when(source != me)
            def _():
                body(lax.rem(me - source + heads_n, heads_n))

        each_chunk(one)

    v_args = (V, v_in, v_ref, FRAME_BLOCKS)
    k_args = (K, k_rows, k_ref, FRAME_BLOCKS)
    q_args = (Q, q_rows, q_ref, 0)
    each_target(lambda offset: exchange(*v_args, offset).start())
    v_own = own_copy(*v_args)
    v_own.start()
    k_load.wait()
    norm_in_place(k_rows, k_gain)
    each_target(lambda offset: exchange(*k_args, offset).start())
    k_own = own_copy(*k_args)
    k_own.start()
    q_load.wait()
    norm_in_place(q_rows, q_gain)
    q_own = own_copy(*q_args)
    q_own.start()
    v_ref[v_ref.shape[0] - 1] = jnp.zeros((BLOCK, width), jnp.bfloat16)
    ones_ref[0] = jnp.ones((BLOCK, HEAD_DIM), jnp.bfloat16)
    ones_ref[1] = jnp.zeros((BLOCK, HEAD_DIM), jnp.bfloat16)

    v_own.wait()
    send_halo(V, v_ref, me)

    def take_v(offset):
        exchange(*v_args, offset).wait_recv()
        send_halo(V, v_ref, lax.rem(me + heads_n - offset, heads_n))

    each_source(take_v)
    k_own.wait()
    send_halo(K, k_ref, me)

    def take_k(offset):
        exchange(*k_args, offset).wait_recv()
        send_halo(K, k_ref, lax.rem(me + heads_n - offset, heads_n))

    relay(V, v_ref)
    each_source(take_k)
    relay(K, k_ref)
    each_target(lambda offset: exchange(*q_args, offset).start())

    def take_halo(chunk):
        @pl.when(halo_comes(chunk))
        def _():
            halo(V, v_ref, chunk).wait_recv()
            halo(K, k_ref, chunk).wait_recv()

    each_chunk(take_halo)
    q_own.wait()
    def attend_part(source):
        def tile(index, carry):
            for more in range(PAIR):
                t = source * part + index * PAIR + more
                attend_tile(q_ref, k_ref, v_ref, ones_ref, o_ref, slots_ref, t, KEEP // GROUP)
            return carry

        lax.fori_loop(0, part // PAIR, tile, 0)

    attend_part(me)
    o_own = pltpu.make_async_copy(
        o_ref.at[part_rows(me)], o_out.at[:, :, part_lanes(me)], own_sems.at[O]
    )
    o_own.start()

    def serve(offset):
        exchange(*q_args, offset).wait_recv()
        attend_part(lax.rem(me + heads_n - offset, heads_n))
        give_back(heads_n - offset).start()

    each_source(serve)

    def finish(offset):
        for args in (v_args, k_args, q_args):
            exchange(*args, offset).wait_send()
        give_back(offset).wait_send()

    each_target(finish)

    def finish_halo(chunk):
        @pl.when(halo_goes(chunk))
        def _():
            halo(V, v_ref, chunk).wait_send()
            halo(K, k_ref, chunk).wait_send()

    each_chunk(finish_halo)
    @pl.when(is_relay)
    def _():
        for which, buffer in ((V, v_ref), (K, k_ref)):
            for index in range(2):
                second_leg(which, buffer, index).wait_send()

    o_own.wait()
    each_target(lambda offset: give_back(offset).wait_recv())


def shards(queries, key_in, values_in, query_gain, key_gain, keep_list, counts):
    groups_n, heads_n = lax.axis_size("tm"), lax.axis_size("head")
    rows, features = queries.shape
    part = rows // BLOCK
    width = features // heads_n
    local_blocks = part * heads_n
    reach = local_blocks + 2 * FRAME_BLOCKS
    first_block = lax.axis_index("tm") * local_blocks - FRAME_BLOCKS
    slots = slot_table(keep_list, counts, first_block, reach)
    scalar = pl.BlockSpec(memory_space=pltpu.SMEM)
    vector = pl.BlockSpec(memory_space=pltpu.VMEM)
    whole = pl.BlockSpec(memory_space=pl.ANY)
    dma = pltpu.SemaphoreType.DMA
    blocks = (part, BLOCK, features)
    bf16 = jnp.bfloat16
    attended = pl.pallas_call(
        functools.partial(whole_kernel, groups_n, heads_n),
        out_shape=jax.ShapeDtypeStruct(blocks, bf16),
        in_specs=[scalar] + [vector] * 2 + [whole] * 3,
        out_specs=whole,
        scratch_shapes=[
            pltpu.VMEM(blocks, bf16),
            pltpu.VMEM(blocks, bf16),
            pltpu.VMEM((local_blocks, BLOCK, width), bf16),
            pltpu.VMEM((reach, BLOCK, width), bf16),
            pltpu.VMEM((reach + 1, BLOCK, width), bf16),
            pltpu.VMEM((local_blocks, BLOCK, width), bf16),
            pltpu.VMEM((2, BLOCK, HEAD_DIM), bf16),
            dma((2,)),
            dma((4,)),
            dma((4, heads_n)),
            dma((4, heads_n)),
            dma((2, heads_n)),
            dma((2, heads_n)),
            pltpu.VMEM((4, part, BLOCK, width), bf16),
            dma((4,)),
            dma((4,)),
        ],
        compiler_params=pltpu.CompilerParams(
            collective_id=0, has_side_effects=True, vmem_limit_bytes=48 * 2**20
        ),
        cost_estimate=pl.CostEstimate(
            flops=local_blocks * BLOCK * KEEP * BLOCK * width * 4,
            bytes_accessed=8 * rows * features,
            transcendentals=local_blocks * BLOCK * KEEP * BLOCK * 2,
        ),
    )(
        slots, query_gain.reshape(1, -1), key_gain.reshape(1, -1),
        queries.reshape(blocks), key_in.reshape(blocks), values_in.reshape(blocks),
    )
    return attended.reshape(rows, features)


def solution(mesh):
    placed = (
        P(("tm", "head"), None),
        P(("tm", "head"), None),
        P(("tm", "head"), None),
        P(),
        P(),
        P("tm", None),
        P("tm"),
    )
    return jax.shard_map(
        shards, mesh=mesh, in_specs=placed, out_specs=P(("tm", "head"), None), check_vma=False
    )
```
